128 devices in a mesh: blk: 64 (over z, y, x), band: 2 (over core).
Axes of the slice: x: 4, y: 4, z: 4, core: 2. Of those that a mesh axis runs over, the one named last changes fastest.
Arguments:
- traces: bfloat16 [4096, 2, 8192], P('blk', None, 'band'), may hold values from -80 to 80
- sources: bfloat16 [128, 2, 8192], P('blk', None, 'band'), may hold values from -80 to 80
- owner: int32 [4096, 1], P('blk'), may hold values from 0 to 63; in each aligned block of 64 rows (0 to 63, 64 to 127, ...) at most 2 rows name the same one
Outputs:
- gathers: float32 [128, 16, 128, 256], P('blk', None, 'band')
The draws below stay inside these ranges and needn't reach their ends.
Inputs may be any that keep to these rules, and one draw needn't show every extreme that they name: Among the 64 stations of one device's rows, at most 2 name the same owner block, and some owner block is named by exactly 2 of them in every draw.
All inputs are finite; a program needn't handle non-finite values.
Results may differ from the reference program's by a relative error of at most 0.017.
Values may be sent and summed in bfloat16 or wider, within the bound.
A program may use at most 128 MiB of HBM per device.

```python
import math
import jax
import jax.numpy as jnp
import numpy as np
from jax import lax

BINS = 8192
DEC = 8
ST_DEV = 64
VS = 2
CAP = 2
RSLOTS = 128
STATIONS = 4096
SOURCES = 128
Q = 16
GROUP_BINS = 4096
OUT = 256
N_BLK = 64
N_BAND = 2


def random_spectrum_rows(key, row_total):
    base_key, scale_key = jax.random.split(key)
    position = jnp.arange(BINS, dtype=jnp.float32) / BINS
    values = jnp.clip(jax.random.normal(base_key, (row_total, 2, BINS), jnp.float32), -5.0, 5.0)
    profile = 1.6 - 1.2 * position
    row_scale = jnp.exp(jax.random.uniform(scale_key, (row_total, 1, 1), jnp.float32) * math.log(10.0))
    return (values * profile[None, None, :] * row_scale).astype(jnp.bfloat16)


def draw_traces(key, part):
    return random_spectrum_rows(jax.random.fold_in(key, 11), STATIONS)


def draw_sources(key, part):
    return random_spectrum_rows(jax.random.fold_in(key, 23), SOURCES)


def shared_out(stream_key, own, number, rows, number_of, top, bound, skew):
    sequence = jax.random.permutation(stream_key, number_of)
    heavy_load, ordinary = load_shares(number_of, rows * top, bound, skew, True), load_shares(number_of, rows * top, bound, skew, False)
    places = jnp.arange(number_of)

    def named(sizes, rotation):
        used = int((sizes > 0).sum())
        fixed = max(1, used // 4)
        passed = fixed + (places - fixed + rotation * (used - fixed)) % max(1, number_of - fixed)
        return jnp.zeros((number_of,), jnp.int32).at[sequence[jnp.where(places < fixed, places, passed)]].set(jnp.asarray(sizes, jnp.int32))

    sizes = jnp.where(number % 4 == 0, named(heavy_load, number // 4), named(ordinary, number - number // 4 - 1))
    mixed = jax.random.permutation(jax.random.fold_in(own, 3), number_of)
    donor, taker = mixed[0:number_of // 2 * 2:2], mixed[1:number_of // 2 * 2:2]
    slack = jnp.minimum(sizes[donor] - 1, bound - sizes[taker]) // 2
    slack = jnp.where((donor == sequence[0]) | (taker == sequence[0]) | (sizes[taker] == 0), 0, jnp.maximum(slack, 0))
    passed = jax.random.randint(jax.random.fold_in(own, 4), (number_of // 2,), 0, 1 << 20) % (slack + 1)
    sizes = sizes.at[donor].add(-passed).at[taker].add(passed)
    items = jnp.searchsorted(jnp.cumsum(sizes), jnp.arange(rows * top), side="right").astype(jnp.int32)
    grid = items.reshape(top, rows).T
    grid = grid[jax.random.permutation(jax.random.fold_in(own, 1), rows)]
    rotation = jax.random.randint(jax.random.fold_in(own, 2), (rows, 1), 0, top)
    return jnp.take_along_axis(grid, (jnp.arange(top)[None, :] + rotation) % top, axis=1)


def load_shares(count, total, reach, lean, full):
    loads = [(1 << 20) // math.isqrt(standing ** lean) + 1 for standing in range(1, count + 1)]
    largest = reach if full else min(reach, max(-(-total // count), total * loads[0] // sum(loads)))
    least = 1 if total - largest >= count - 1 else 0
    holding, surplus = [largest] + [least] * (count - 1), total - largest - least * (count - 1)
    while surplus > 0:
        movable = [i for i in range(1, count) if holding[i] < largest] or [i for i in range(1, count) if holding[i] < reach]
        pool, budget = sum([loads[i] for i in movable]), surplus
        for i in movable:
            more = min(reach - holding[i], max(1, budget * loads[i] // pool), surplus)
            holding[i] = holding[i] + more
            surplus = surplus - more
    return np.array(holding)


def setup_inputs(seed: int = 0) -> dict:
    key_list = jax.random.split(jax.random.key(seed), 4)
    traces = draw_traces(jax.random.fold_in(key_list[3], 71), 0)
    sources = draw_sources(jax.random.fold_in(key_list[3], 71), 0)
    owner_keys = jax.random.split(jax.random.fold_in(key_list[2], 1), STATIONS // ST_DEV)
    owner_turns = jax.random.permutation(jax.random.fold_in(key_list[2], 3), STATIONS // ST_DEV)
    owner = jax.vmap(lambda own, number: shared_out(jax.random.fold_in(key_list[2], 2), own, number, ST_DEV, N_BLK, 1, CAP, 2))(owner_keys, owner_turns).reshape((STATIONS, 1))
    return {"traces": traces, "sources": sources, "owner": owner}


EPS = 1e-06

def whiten(spectrum_rows):
    values = spectrum_rows.astype(jnp.float32)
    power = lax.optimization_barrier(jnp.mean(values * values, axis=(1, 2)))
    return (values * lax.rsqrt(power + EPS)[:, None, None]).astype(jnp.bfloat16)

def reference(traces, sources, owner):
    white_traces = whiten(traces)
    white_sources = whiten(sources)
    owner_flat = owner[:, 0].astype(jnp.int32)
    owner_blocks = owner_flat.reshape(N_BLK, ST_DEV)
    owner_hits = (owner_blocks[:, :, None] == jnp.arange(N_BLK, dtype=jnp.int32)[None, None, :]).astype(jnp.int32)
    earlier = jnp.cumsum(owner_hits, axis=1) - owner_hits
    arrival = lax.optimization_barrier(jnp.sum(owner_hits * earlier, axis=2))
    slot_index = (jnp.arange(N_BLK, dtype=jnp.int32)[:, None] * CAP + arrival).reshape(-1).astype(jnp.int32)
    resident = jnp.zeros((N_BLK, RSLOTS, 2, BINS), jnp.bfloat16).at[owner_flat, slot_index].set(white_traces)
    bin_index = jnp.arange(BINS, dtype=jnp.int32)
    lag_value = (jnp.arange(OUT, dtype=jnp.int32) - OUT // 2) * DEC
    phase_angle = jnp.mod(bin_index[:, None] * lag_value[None, :], BINS).astype(jnp.float32) * (2.0 * math.pi / BINS)
    cosine_table = jnp.cos(phase_angle)
    sine_table = jnp.sin(phase_angle)
    norm_scale = BINS ** (-0.5)

    def per_block(block_index):
        chosen = lax.dynamic_slice_in_dim(white_sources, (block_index * VS).astype(jnp.int32), VS, 0).astype(jnp.float32)
        real_part = chosen[:, 0][:, :, None]
        imag_part = chosen[:, 1][:, :, None]
        kernel_real = (real_part * cosine_table[None] + imag_part * sine_table[None]) * norm_scale
        kernel_imag = (imag_part * cosine_table[None] - real_part * sine_table[None]) * norm_scale
        kernel = jnp.stack([kernel_real, kernel_imag], axis=1).astype(jnp.bfloat16)
        kernel = lax.optimization_barrier(kernel).astype(jnp.float32).reshape(VS, 2, N_BAND, GROUP_BINS, OUT)

        def per_offset(offset):
            visitor_index = jnp.mod(block_index - offset, N_BLK).astype(jnp.int32)
            visitor = lax.dynamic_index_in_dim(resident, visitor_index, 0, keepdims=False)
            visitor = visitor.astype(jnp.float32).reshape(RSLOTS, 2, N_BAND, GROUP_BINS)
            partial_value = jnp.einsum('rcgk,scgkl->gsrl', visitor, kernel)
            partial_value = lax.optimization_barrier(partial_value.astype(jnp.bfloat16)).astype(jnp.float32)
            return lax.optimization_barrier(jnp.sum(partial_value, axis=0))
        result = lax.map(per_offset, jnp.arange(Q, dtype=jnp.int32))
        return jnp.transpose(result, (1, 0, 2, 3))
    gathered = lax.map(per_block, jnp.arange(N_BLK, dtype=jnp.int32))
    return gathered.reshape(SOURCES, Q, RSLOTS, OUT)
```

```python
import functools
import math

import jax
import jax.numpy as jnp
import numpy as np
from jax import lax
from jax.experimental import pallas as pl
from jax.experimental.pallas import tpu as pltpu
from jax.sharding import PartitionSpec as P

BINS = 8192
DEC = 8
OUT = 256
EPS = 1e-06
Q = 16
PERIOD = BINS // DEC
LANES = 128
SIDE = 4
ROWS = BINS // LANES
GROUP = 8
PARTS = ((0, 48), (48, 96), (96, 128))
ORDERS = ((2, 1, 0), (1, 0, 2), (0, 2, 1))


def lag_table():
    bins = np.arange(PERIOD)[:, None]
    lags = np.arange(OUT)[None, :] - OUT // 2
    angle = 2.0 * np.pi * ((bins * lags) % PERIOD) / PERIOD
    shape = (PERIOD // LANES, LANES, OUT)
    both = [np.cos(angle).reshape(shape), np.sin(angle).reshape(shape)]
    return (np.concatenate(both, axis=1) / math.sqrt(BINS)).astype(jnp.bfloat16)


def whiten(block):
    values = block.astype(jnp.float32)
    total = jnp.sum(jnp.sum(values * values, axis=0, keepdims=True), axis=1, keepdims=True)
    return (values * lax.rsqrt(total / (2 * BINS) + EPS)).astype(jnp.bfloat16)


def fused(
    idx,
    x_in,
    s_in,
    table,
    recv,
    xs,
    raw,
    sb,
    ca,
    cb,
    stage,
    pair_send,
    pair_recv,
    local_sem,
    ring_send,
    ring_recv,
    out_send,
    out_recv,
    twin_send,
):
    blk = lax.axis_index("blk")
    band = lax.axis_index("band")
    blocks = SIDE**3
    stations = x_in.shape[0]
    half = ROWS // 2
    place = [blk // 16, (blk // 4) % 4, blk % 4]

    def device(coords, core):
        return ((coords[0] * SIDE + coords[1]) * SIDE + coords[2], core)

    def remote(src, dst, send, recv_sem, target):
        return pltpu.make_async_remote_copy(
            src_ref=src,
            dst_ref=dst,
            send_sem=send,
            recv_sem=recv_sem,
            device_id=target,
            device_id_type=pl.DeviceIdType.MESH,
        )

    mine = pl.ds(pl.multiple_of(band * half, half), half)
    other = pl.ds(pl.multiple_of((1 - band) * half, half), half)
    twin = (blk, 1 - band)

    source_out = remote(
        s_in.at[1 - band], raw.at[:, mine, :], pair_send.at[0], pair_recv.at[0], twin
    )
    source_out.start()
    source_keep = pltpu.make_async_copy(s_in.at[band], raw.at[:, mine, :], local_sem.at[0])
    source_keep.start()
    station_out = remote(
        x_in, xs.at[pl.ds(0, stations), :, mine, :], pair_send.at[1], pair_recv.at[1], twin
    )
    station_out.start()
    station_keep = pltpu.make_async_copy(
        x_in, xs.at[pl.ds(0, stations), :, mine, :], local_sem.at[1]
    )
    station_keep.start()
    xs[stations] = jnp.zeros(xs.shape[1:], xs.dtype)

    source_keep.wait()
    source_out.wait_recv()
    source = raw[...].reshape(2 * ROWS, LANES)
    sb[place[0], place[1], place[2]] = whiten(source)

    pending = [source_out, station_out]

    def region(coords, rows):
        return sb.at[tuple(coords) + (pl.ds(rows[0], rows[1] - rows[0]), slice(None))]

    def moved(axis, step):
        coords = list(place)
        coords[axis] = (coords[axis] + step) % SIDE
        return coords

    def held(part, level):
        coords = list(place)
        for axis in ORDERS[part][:level]:
            coords[axis] = slice(None)
        return coords

    def ring_copy(part, level, way, coords, step):
        axis = ORDERS[part][level]
        spot = (part * 3 + level) * 4 + way
        return remote(
            region(coords, PARTS[part]),
            region(coords, PARTS[part]),
            ring_send.at[spot],
            ring_recv.at[spot],
            device(moved(axis, step), band),
        )

    def with_axis(coords, axis, value):
        coords = list(coords)
        coords[axis] = value
        return coords

    def start_level(part, level):
        coords = held(part, level)
        steps = (1, -1, 2) if level < 2 else (1, -1)
        for way, step in enumerate(steps):
            copy = ring_copy(part, level, way, coords, step)
            copy.start()
            pending.append(copy)

    def wait_way(part, level, way, step, half_axis=None, half_at=None):
        axis = ORDERS[part][level]
        coords = with_axis(held(part, level), axis, (place[axis] + step) % SIDE)
        if half_axis is not None:
            coords[half_axis] = pl.ds(half_at, SIDE // 2)
        ring_copy(part, level, way, coords, 1).wait_recv()

    for part in range(3):
        start_level(part, 0)
    for level in (0, 1):
        for part in range(3):
            for way, step in enumerate((-1, 1, 2)):
                wait_way(part, level, way, step)
            start_level(part, level + 1)

    station_keep.wait()
    station_out.wait_recv()

    @pl.loop(0, stations)
    def _(i):
        xs[i] = whiten(xs[i].reshape(2 * ROWS, LANES)).reshape(2, ROWS, LANES)

    for part in range(3):
        axis = ORDERS[part][2]
        split = ORDERS[part][0]
        for way, (come, go, at) in enumerate(((-1, 1, 0), (1, -1, 2))):
            wait_way(part, 2, way, come)
            coords = with_axis(held(part, 2), axis, (place[axis] + come) % SIDE)
            coords[split] = pl.ds(at, SIDE // 2)
            copy = ring_copy(part, 2, 2 + way, coords, go)
            copy.start()
            pending.append(copy)
    for part in range(3):
        split = ORDERS[part][0]
        wait_way(part, 2, 2, 2, split, 0)
        wait_way(part, 2, 3, 2, split, 2)

    side = blk // (blocks // 2)
    row = blk % (blocks // 2)

    def target(turn):
        coords = [
            (place[0] + turn // 16) % SIDE,
            (place[1] + (turn // 4) % 4) % SIDE,
            (place[2] + turn % 4) % SIDE,
        ]
        return coords, (coords[0] * SIDE + coords[1]) * SIDE + coords[2]

    @pl.loop(0, blocks // GROUP)
    def _(group):
        @pl.loop(0, GROUP)
        def _(member):
            coords, a = target(group * GROUP + member)
            real = sb[coords[0], coords[1], coords[2], pl.ds(0, ROWS), :]
            imag = sb[coords[0], coords[1], coords[2], pl.ds(ROWS, ROWS), :]

            @pl.loop(0, 2 * Q, unroll=4)
            def _(slot):
                b = (a + blocks - slot % Q) % blocks
                i = idx[(slot // Q) * blocks + b]
                xr = xs[i, 0]
                xi = xs[i, 1]
                at = pl.ds(pl.multiple_of((member * 2 * Q + slot) * 8, 8), 8)
                for out, prod in ((ca, xr * real + xi * imag), (cb, xr * imag - xi * real)):
                    fold = (prod[0:16] + prod[16:32]) + (prod[32:48] + prod[48:64])
                    fold = fold.astype(jnp.float32)
                    out[at, :] = fold[0:8] + fold[8:16]

        lags = jnp.zeros((GROUP * 2 * Q, OUT), jnp.float32)
        for k in range(PERIOD // LANES):
            pick = pl.ds(k, GROUP * 2 * Q, stride=8)
            left = jnp.concatenate([ca[pick, :], cb[pick, :]], axis=1).astype(jnp.bfloat16)
            lags += jnp.dot(left, table[k], preferred_element_type=jnp.float32)
        stage[pl.ds(group * GROUP, GROUP)] = lags.astype(jnp.bfloat16).reshape(GROUP, 2 * Q, OUT)

        @pl.loop(0, GROUP)
        def _(member):
            turn = group * GROUP + member
            _, a = target(turn)

            @pl.when(turn > 0)
            def _():
                remote(
                    stage.at[turn], recv.at[row, band], out_send, out_recv, (a, side)
                ).start()

    @pl.when(side == band)
    def _():
        pltpu.make_async_copy(stage.at[0], recv.at[row, band], out_recv).start()

    @pl.when(side != band)
    def _():
        copy = remote(stage.at[0], recv.at[row, band], twin_send, out_recv, twin)
        copy.start()
        copy.wait_send()

    for copy in pending:
        copy.wait_send()
    pltpu.make_async_copy(
        stage.at[pl.ds(1, blocks - 1)], stage.at[pl.ds(1, blocks - 1)], out_send
    ).wait()
    pltpu.make_async_copy(recv, recv, out_recv).wait()


def unscramble(recv, out):
    for c in range(recv.shape[0]):
        value = recv[c, 0].astype(jnp.float32)
        for arrival in range(2):
            out[pl.ds(2 * c + arrival, Q, stride=64), :] = value[arrival * Q : (arrival + 1) * Q]


def per_device(traces, sources, owner):
    stations = traces.shape[0]
    blocks = lax.axis_size("blk")
    x_in = traces.reshape(stations, 2, ROWS // 2, LANES)
    s_in = sources.reshape(2, 2, ROWS // 2, LANES)
    owners = owner[:, 0]
    hits = owners[None, :] == jnp.arange(blocks, dtype=jnp.int32)[:, None]
    numbers = jnp.arange(stations, dtype=jnp.int32)[None, :]
    first = jnp.min(jnp.where(hits, numbers, stations), axis=1)
    last = jnp.max(jnp.where(hits, numbers, -1), axis=1)
    idx = jnp.concatenate([first, jnp.where(last > first, last, stations)])
    table = jnp.asarray(lag_table())
    vmem = pl.BlockSpec(memory_space=pltpu.VMEM)
    recv = pl.pallas_call(
        fused,
        out_shape=jax.ShapeDtypeStruct((blocks // 2, 2, 2 * Q, OUT), jnp.bfloat16),
        in_specs=[
            pl.BlockSpec(memory_space=pltpu.SMEM),
            pl.BlockSpec(memory_space=pl.ANY),
            pl.BlockSpec(memory_space=pl.ANY),
            vmem,
        ],
        out_specs=vmem,
        scratch_shapes=[
            pltpu.VMEM((stations + 1, 2, ROWS, LANES), jnp.bfloat16),
            pltpu.VMEM((2, ROWS, LANES), jnp.bfloat16),
            pltpu.VMEM((SIDE, SIDE, SIDE, 2 * ROWS, LANES), jnp.bfloat16),
            pltpu.VMEM((GROUP * 2 * Q * 8, LANES), jnp.float32),
            pltpu.VMEM((GROUP * 2 * Q * 8, LANES), jnp.float32),
            pltpu.VMEM((blocks, 2 * Q, OUT), jnp.bfloat16),
            pltpu.SemaphoreType.DMA((2,)),
            pltpu.SemaphoreType.DMA((2,)),
            pltpu.SemaphoreType.DMA((2,)),
            pltpu.SemaphoreType.DMA((36,)),
            pltpu.SemaphoreType.DMA((36,)),
            pltpu.SemaphoreType.DMA,
            pltpu.SemaphoreType.DMA,
            pltpu.SemaphoreType.DMA,
        ],
        compiler_params=pltpu.CompilerParams(
            has_side_effects=True, vmem_limit_bytes=40 * 1024 * 1024
        ),
        name="correlate",
    )(idx, x_in, s_in, table)
    out = pl.pallas_call(
        unscramble,
        grid=(2, 2),
        out_shape=jax.ShapeDtypeStruct((2 * Q * 64, OUT), jnp.float32),
        in_specs=[pl.BlockSpec((blocks // 2, 1, 2 * Q, LANES), lambda s, l: (0, s, 0, l))],
        out_specs=pl.BlockSpec((Q * 64, LANES), lambda s, l: (s, l)),
        name="unscramble",
    )(recv)
    return out.reshape(2, Q, 64, OUT)


def solution(mesh):
    placed = (P("blk", None, "band"), P("blk", None, "band"), P("blk", None))
    return jax.shard_map(
        per_device,
        mesh=mesh,
        in_specs=placed,
        out_specs=P("blk", None, "band", None),
        check_vma=False,
    )
```

```python
import math

import jax
import jax.numpy as jnp
import numpy as np
from jax import lax
from jax.experimental import pallas as pl
from jax.experimental.pallas import tpu as pltpu
from jax.sharding import PartitionSpec as P

BINS = 8192
DEC = 8
OUT = 256
EPS = 1e-06
Q = 16
PERIOD = BINS // DEC
LANES = 128
SIDE = 4
ROWS = BINS // LANES
GROUP = 8
PATH = (
    ((0, 0), None),
    ((1, 0), (1, 0)),
    ((3, 0), (3, 0)),
    ((0, 1), (0, 1)),
    ((0, 3), (0, 3)),
    ((1, 1), (1, 0)),
    ((3, 3), (3, 0)),
    ((3, 1), (0, 1)),
    ((1, 3), (0, 3)),
    ((2, 0), (1, 0)),
    ((2, 1), (3, 0)),
    ((0, 2), (0, 1)),
    ((1, 2), (0, 3)),
    ((2, 2), (1, 0)),
    ((3, 2), (3, 0)),
    ((2, 3), (0, 3)),
)
ROUNDS = {1: range(1, 5), 4: range(5, 9), 7: range(9, 13), 10: range(13, 16)}


def lag_table():
    bins = np.arange(PERIOD)[:, None]
    lags = np.arange(OUT)[None, :] - OUT // 2
    angle = 2.0 * np.pi * ((bins * lags) % PERIOD) / PERIOD
    shape = (PERIOD // LANES, LANES, OUT)
    both = [np.cos(angle).reshape(shape), np.sin(angle).reshape(shape)]
    return (np.concatenate(both, axis=1) / math.sqrt(BINS)).astype(jnp.bfloat16)


def whiten(values):
    total = jnp.sum(jnp.sum(values * values, axis=(0, 1), keepdims=True), axis=2, keepdims=True)
    return (values * lax.rsqrt(total / (2 * BINS) + EPS)).astype(jnp.bfloat16)


def fold(products):
    pairs = (products[0:16] + products[16:32]) + (products[32:48] + products[48:64])
    pairs = pairs.astype(jnp.float32)
    return pairs[0:8] + pairs[8:16]


def correlate(
    idx,
    x_in,
    s_in,
    table,
    recv,
    raw,
    xs,
    source,
    sb,
    ca,
    cb,
    stage,
    pair_send,
    pair_recv,
    local_sem,
    ring_send,
    ring_recv,
    out_send,
    out_recv,
    twin_send,
):
    blk = lax.axis_index("blk")
    band = lax.axis_index("band")
    blocks = SIDE**3
    stations = x_in.shape[0]
    half = ROWS // 2
    pz, py, px = blk // 16, (blk // 4) % 4, blk % 4
    twin = (blk, 1 - band)

    def device(dy, dz, dx):
        z, y, x = (pz + dz) & 3, (py + dy) & 3, (px + dx) & 3
        return ((z * SIDE + y) * SIDE + x, band)

    def remote(src, dst, send, recv_sem, target):
        return pltpu.make_async_remote_copy(
            src_ref=src,
            dst_ref=dst,
            send_sem=send,
            recv_sem=recv_sem,
            device_id=target,
            device_id_type=pl.DeviceIdType.MESH,
        )

    barrier = pltpu.get_barrier_semaphore()
    greeted = [twin]
    for step in (1, 2, 3):
        greeted += [device(step, 0, 0), device(0, step, 0), device(0, 0, step)]
    greeted = [g for n, g in enumerate(greeted) if n not in (4, 5)]
    for target in greeted:
        pl.semaphore_signal(barrier, inc=1, device_id=target, device_id_type=pl.DeviceIdType.MESH)

    mine = pl.ds(pl.multiple_of(band * half, half), half)
    source_keep = pltpu.make_async_copy(s_in.at[band], source.at[:, mine, :], local_sem.at[0])
    source_keep.start()
    station_keep = pltpu.make_async_copy(x_in, raw.at[:, :, mine, :], local_sem.at[1])
    station_keep.start()
    xs[stations] = jnp.zeros(xs.shape[1:], xs.dtype)
    pl.semaphore_wait(barrier, len(greeted))

    source_out = remote(
        s_in.at[1 - band], source.at[:, mine, :], pair_send.at[0], pair_recv.at[0], twin
    )
    source_out.start()
    station_out = remote(x_in, raw.at[:, :, mine, :], pair_send.at[1], pair_recv.at[1], twin)
    station_out.start()
    source_keep.wait()
    source_out.wait_recv()
    own = whiten(source[...].astype(jnp.float32))
    sb[pz, py, px] = own.reshape(2 * ROWS, LANES)
    pending = [source_out, station_out]

    def x_copy(step, at):
        block = sb.at[pz, py, at]
        return remote(
            block, block, ring_send.at[15 + step - 1], ring_recv.at[15 + step - 1], device(0, 0, step)
        )

    for step in (1, 3, 2):
        copy = x_copy(step, px)
        copy.start()
        pending.append(copy)
    for step in (1, 3, 2):
        x_copy(step, (px + 4 - step) & 3).wait_recv()

    def row_copy(n, place):
        row = sb.at[(pz + 4 - place[1]) & 3, (py + 4 - place[0]) & 3]
        step = PATH[n][1]
        return remote(
            row, row, ring_send.at[n - 1], ring_recv.at[n - 1], device(step[0], step[1], 0)
        )

    def pass_on(n):
        place = PATH[n][0]
        for child in range(1, 16):
            there, step = PATH[child]
            if ((there[0] - step[0]) % 4, (there[1] - step[1]) % 4) == place:
                row_copy(child, place).start()

    pass_on(0)

    station_keep.wait()
    station_out.wait_recv()

    @pl.loop(0, stations // 8)
    def _(group):
        for member in range(8):
            i = group * 8 + member
            white = whiten(raw[i].astype(jnp.float32))
            xs[i, 0:2] = white
            xs[i, 2] = white[0] + white[1]

    side = blk // (blocks // 2)
    row = blk % (blocks // 2)

    def block_at(turn):
        n, x = turn // SIDE, turn % SIDE
        dy, dz = 0, 0
        for k in range(1, 16):
            (ky, kz), _ = PATH[k]
            dy += jnp.where(n == k, ky, 0)
            dz += jnp.where(n == k, kz, 0)
        return (pz + 4 - dz) & 3, (py + 4 - dy) & 3, (px + x) & 3

    @pl.loop(0, blocks // SIDE)
    def _(n):
        for when, arrivals in ROUNDS.items():

            @pl.when(n == when)
            def _():
                for k in arrivals:
                    row_copy(k, PATH[k][0]).wait_recv()
                    pass_on(k)

        @pl.loop(0, SIDE)
        def _(x):
            az, ay, ax = block_at(n * SIDE + x)
            a = (az * SIDE + ay) * SIDE + ax
            real = sb[az, ay, ax, pl.ds(0, ROWS), :]
            imag = sb[az, ay, ax, pl.ds(ROWS, ROWS), :]
            less = real - imag
            more = real + imag
            base = ((n % 2) * SIDE + x) * (2 * Q * 8)
            for slot in range(2 * Q):
                i = idx[(slot // Q) * blocks + ((a + blocks - slot % Q) & (blocks - 1))]
                k1 = fold(xs[i, 2] * imag)
                k2 = fold(xs[i, 0] * less)
                k3 = fold(xs[i, 1] * more)
                at = pl.ds(pl.multiple_of(base + slot * 8, 8), 8)
                ca[at, :] = k1 + k2
                cb[at, :] = k1 - k3

        @pl.when(n % 2 == 1)
        def _():
            lags = jnp.zeros((GROUP * 2 * Q, OUT), jnp.float32)
            for k in range(PERIOD // LANES):
                pick = pl.ds(k, GROUP * 2 * Q, stride=8)
                left = jnp.concatenate([ca[pick, :], cb[pick, :]], axis=1).astype(jnp.bfloat16)
                lags += jnp.dot(left, table[k], preferred_element_type=jnp.float32)
            first = (n // 2) * GROUP
            stage[pl.ds(first, GROUP)] = lags.astype(jnp.bfloat16).reshape(GROUP, 2 * Q, OUT)

            @pl.loop(0, GROUP)
            def _(member):
                turn = first + member
                az, ay, ax = block_at(turn)

                @pl.when(turn > 0)
                def _():
                    remote(
                        stage.at[turn],
                        recv.at[row, band],
                        out_send,
                        out_recv,
                        ((az * SIDE + ay) * SIDE + ax, side),
                    ).start()

    @pl.when(side == band)
    def _():
        pltpu.make_async_copy(stage.at[0], recv.at[row, band], out_recv).start()

    @pl.when(side != band)
    def _():
        copy = remote(stage.at[0], recv.at[row, band], twin_send, out_recv, twin)
        copy.start()
        copy.wait_send()

    for copy in pending:
        copy.wait_send()
    for n in range(1, 16):
        row_copy(n, PATH[n][0]).wait_send()
    pltpu.make_async_copy(
        stage.at[pl.ds(1, blocks - 1)], stage.at[pl.ds(1, blocks - 1)], out_send
    ).wait()
    pltpu.make_async_copy(recv, recv, out_recv).wait()


def unscramble(recv, out, wide, sem):
    to = lax.broadcasted_iota(jnp.int32, (256, 256), 0)
    at = lax.broadcasted_iota(jnp.int32, (256, 256), 1)
    move = ((to % 16) * 16 + to // 16 == at).astype(jnp.bfloat16)
    copies = []
    for s in range(2):
        for g in range(4):
            value = recv[8 * g : 8 * g + 8, s].reshape(256, OUT)
            value = jnp.dot(move, value, preferred_element_type=jnp.float32)
            wide[s, :, 16 * g : 16 * g + 16, :] = value.reshape(Q, 16, OUT)
        copy = pltpu.make_async_copy(wide.at[s], out.at[s], sem.at[s])
        copy.start()
        copies.append(copy)
    for copy in copies:
        copy.wait()


def per_device(traces, sources, owner):
    stations = traces.shape[0]
    blocks = lax.axis_size("blk")
    x_in = traces.reshape(stations, 2, ROWS // 2, LANES)
    s_in = sources.reshape(2, 2, ROWS // 2, LANES)
    owners = owner[:, 0]
    hits = owners[None, :] == jnp.arange(blocks, dtype=jnp.int32)[:, None]
    numbers = jnp.arange(stations, dtype=jnp.int32)[None, :]
    first = jnp.min(jnp.where(hits, numbers, stations), axis=1)
    last = jnp.max(jnp.where(hits, numbers, -1), axis=1)
    idx = jnp.concatenate([first, jnp.where(last > first, last, stations)])
    table = jnp.asarray(lag_table())
    vmem = pl.BlockSpec(memory_space=pltpu.VMEM)
    recv = pl.pallas_call(
        correlate,
        out_shape=jax.ShapeDtypeStruct((blocks // 2, 2, 2 * Q, OUT), jnp.bfloat16),
        in_specs=[
            pl.BlockSpec(memory_space=pltpu.SMEM),
            pl.BlockSpec(memory_space=pl.ANY),
            pl.BlockSpec(memory_space=pl.ANY),
            vmem,
        ],
        out_specs=vmem,
        scratch_shapes=[
            pltpu.VMEM((stations, 2, ROWS, LANES), jnp.bfloat16),
            pltpu.VMEM((stations + 1, 3, ROWS, LANES), jnp.bfloat16),
            pltpu.VMEM((2, ROWS, LANES), jnp.bfloat16),
            pltpu.VMEM((SIDE, SIDE, SIDE, 2 * ROWS, LANES), jnp.bfloat16),
            pltpu.VMEM((GROUP * 2 * Q * 8, LANES), jnp.float32),
            pltpu.VMEM((GROUP * 2 * Q * 8, LANES), jnp.float32),
            pltpu.VMEM((blocks, 2 * Q, OUT), jnp.bfloat16),
            pltpu.SemaphoreType.DMA((2,)),
            pltpu.SemaphoreType.DMA((2,)),
            pltpu.SemaphoreType.DMA((2,)),
            pltpu.SemaphoreType.DMA((18,)),
            pltpu.SemaphoreType.DMA((18,)),
            pltpu.SemaphoreType.DMA,
            pltpu.SemaphoreType.DMA,
            pltpu.SemaphoreType.DMA,
        ],
        compiler_params=pltpu.CompilerParams(
            has_side_effects=True, collective_id=0, vmem_limit_bytes=40 * 1024 * 1024
        ),
        name="correlate",
    )(idx, x_in, s_in, table)
    return pl.pallas_call(
        unscramble,
        out_shape=jax.ShapeDtypeStruct((2, Q, 64, OUT), jnp.float32),
        in_specs=[vmem],
        out_specs=pl.BlockSpec(memory_space=pl.ANY),
        scratch_shapes=[
            pltpu.VMEM((2, Q, 64, OUT), jnp.float32),
            pltpu.SemaphoreType.DMA((2,)),
        ],
        name="unscramble",
    )(recv)


def solution(mesh):
    placed = (P("blk", None, "band"), P("blk", None, "band"), P("blk", None))
    return jax.shard_map(
        per_device,
        mesh=mesh,
        in_specs=placed,
        out_specs=P("blk", None, "band", None),
        check_vma=False,
    )
```

```python
import math

import jax
import jax.numpy as jnp
import numpy as np
from jax import lax
from jax.experimental import pallas as pl
from jax.experimental.pallas import tpu as pltpu
from jax.sharding import PartitionSpec as P

BINS = 8192
DEC = 8
OUT = 256
EPS = 1e-06
Q = 16
PERIOD = BINS // DEC
LANES = 128
SIDE = 4
ROWS = BINS // LANES
GROUP = 8
PATH = (
    ((0, 0), None),
    ((1, 0), (1, 0)),
    ((3, 0), (3, 0)),
    ((0, 1), (0, 1)),
    ((0, 3), (0, 3)),
    ((1, 1), (1, 0)),
    ((3, 3), (3, 0)),
    ((0, 2), (0, 1)),
    ((1, 3), (0, 3)),
    ((2, 0), (1, 0)),
    ((3, 1), (3, 0)),
    ((1, 2), (0, 1)),
    ((2, 1), (1, 0)),
    ((2, 3), (3, 0)),
    ((2, 2), (1, 0)),
    ((3, 2), (3, 0)),
)
ROUNDS = {1: range(1, 5), 4: range(5, 9), 7: range(9, 12), 10: range(12, 14), 13: range(14, 16)}


def lag_table():
    bins = np.arange(PERIOD)[:, None]
    lags = np.arange(OUT)[None, :] - OUT // 2
    angle = 2.0 * np.pi * ((bins * lags) % PERIOD) / PERIOD
    shape = (PERIOD // LANES, LANES, OUT)
    both = [np.cos(angle).reshape(shape), np.sin(angle).reshape(shape)]
    return (np.concatenate(both, axis=1) / math.sqrt(BINS)).astype(jnp.bfloat16)


def whiten(block, wide):
    values = block.astype(jnp.float32)
    total = jnp.sum(jnp.sum(values * values, axis=0, keepdims=True), axis=1, keepdims=True)
    wide[...] = values * lax.rsqrt(total / (2 * BINS) + EPS)
    return [wide[pl.ds(part, ROWS, stride=2), :].astype(jnp.bfloat16) for part in range(2)]


def find_slots(owner, found):
    stations = owner.shape[1]
    shape = (stations, stations)
    j = lax.broadcasted_iota(jnp.int32, shape, 0)
    b = lax.broadcasted_iota(jnp.int32, shape, 1)
    named = jnp.sum(jnp.where(j == b, owner[...], 0), axis=1, keepdims=True)
    hits = named == b
    first = jnp.min(jnp.where(hits, j, stations), axis=0, keepdims=True)
    last = jnp.max(jnp.where(hits, j, -1), axis=0, keepdims=True)
    found[0:1, 0:stations] = first
    found[1:2, 0:stations] = jnp.where(last > first, last, stations)


def fold(products):
    pairs = (products[0:16] + products[16:32]) + (products[32:48] + products[48:64])
    pairs = pairs.astype(jnp.float32)
    return pairs[0:8] + pairs[8:16]


def correlate(
    owner,
    x_in,
    s_in,
    table_in,
    recv,
    table,
    found,
    idx,
    wide,
    raw,
    xs,
    source,
    sb,
    ca,
    cb,
    stage,
    pair_send,
    pair_recv,
    local_sem,
    ring_send,
    ring_recv,
    out_send,
    out_recv,
    twin_send,
):
    blk = lax.axis_index("blk")
    band = lax.axis_index("band")
    blocks = SIDE**3
    stations = x_in.shape[0]
    twin = (blk, 1 - band)
    size_u = jnp.where(band == 0, SIDE, 1)
    size_r = jnp.where(band == 0, 1, SIDE)
    px, py, pv = blk % SIDE, (blk // SIDE) % SIDE, blk // (SIDE * SIDE)
    pr = jnp.where(band == 0, px, py)
    pu = jnp.where(band == 0, py, px)

    def number(v, u, r):
        return v * (SIDE * SIDE) + u * size_u + r * size_r

    def device(du, dv, dr):
        return (number((pv + dv) & 3, (pu + du) & 3, (pr + dr) & 3), band)

    def remote(src, dst, send, recv_sem, target):
        return pltpu.make_async_remote_copy(
            src_ref=src,
            dst_ref=dst,
            send_sem=send,
            recv_sem=recv_sem,
            device_id=target,
            device_id_type=pl.DeviceIdType.MESH,
        )

    barrier = pltpu.get_barrier_semaphore()
    greeted = [twin]
    for step in (1, 2, 3):
        greeted += [device(step, 0, 0), device(0, step, 0), device(0, 0, step)]
    greeted = [g for n, g in enumerate(greeted) if n not in (4, 5)]
    for target in greeted:
        pl.semaphore_signal(barrier, inc=1, device_id=target, device_id_type=pl.DeviceIdType.MESH)

    mine = pl.ds(pl.multiple_of(band * ROWS, ROWS), ROWS)
    source_keep = pltpu.make_async_copy(s_in.at[band], source.at[mine, :], local_sem.at[0])
    source_keep.start()
    station_keep = pltpu.make_async_copy(x_in, raw.at[:, mine, :], local_sem.at[1])
    station_keep.start()
    table_copy = pltpu.make_async_copy(table_in, table, local_sem.at[3])
    table_copy.start()
    find_slots(owner, found)
    index_copy = pltpu.make_async_copy(found, idx, local_sem.at[2])
    index_copy.start()
    xs[stations] = jnp.zeros(xs.shape[1:], xs.dtype)
    pl.semaphore_wait(barrier, len(greeted))

    source_out = remote(
        s_in.at[1 - band], source.at[mine, :], pair_send.at[0], pair_recv.at[0], twin
    )
    source_out.start()
    station_out = remote(x_in, raw.at[:, mine, :], pair_send.at[1], pair_recv.at[1], twin)
    station_out.start()
    source_keep.wait()
    source_out.wait_recv()
    own = whiten(source[...], wide.at[0])
    for part in range(2):
        sb[pv, pu, pr, part * ROWS : (part + 1) * ROWS] = own[part]
    pending = [source_out, station_out]

    def r_copy(step, at):
        block = sb.at[pv, pu, at]
        return remote(
            block, block, ring_send.at[15 + step - 1], ring_recv.at[15 + step - 1], device(0, 0, step)
        )

    for step in (1, 3, 2):
        copy = r_copy(step, pr)
        copy.start()
        pending.append(copy)
    for step in (1, 3, 2):
        r_copy(step, (pr + 4 - step) & 3).wait_recv()

    def row_copy(n, place):
        row = sb.at[(pv + 4 - place[1]) & 3, (pu + 4 - place[0]) & 3]
        step = PATH[n][1]
        return remote(
            row, row, ring_send.at[n - 1], ring_recv.at[n - 1], device(step[0], step[1], 0)
        )

    def pass_on(n):
        place = PATH[n][0]
        for child in range(1, 16):
            there, step = PATH[child]
            if ((there[0] - step[0]) % 4, (there[1] - step[1]) % 4) == place:
                row_copy(child, place).start()

    pass_on(0)
    index_copy.wait()
    table_copy.wait()

    station_keep.wait()
    station_out.wait_recv()

    @pl.loop(0, stations // 8)
    def _(group):
        for member in range(8):
            i = group * 8 + member
            real, imag = whiten(raw[i], wide.at[member])
            xs[i, 0] = real
            xs[i, 1] = imag
            xs[i, 2] = real + imag

    side = blk // (blocks // 2)
    row = blk % (blocks // 2)

    def block_at(turn):
        n, r = turn // SIDE, turn % SIDE
        du, dv = 0, 0
        for k in range(1, 16):
            (ku, kv), _ = PATH[k]
            du += jnp.where(n == k, ku, 0)
            dv += jnp.where(n == k, kv, 0)
        return (pv + 4 - dv) & 3, (pu + 4 - du) & 3, (pr + r) & 3

    @pl.loop(0, blocks // SIDE)
    def _(n):
        for when, arrivals in ROUNDS.items():

            @pl.when(n == when)
            def _():
                for k in arrivals:
                    row_copy(k, PATH[k][0]).wait_recv()
                    pass_on(k)

        @pl.loop(0, SIDE)
        def _(r):
            av, au, ar = block_at(n * SIDE + r)
            a = number(av, au, ar)
            real = sb[av, au, ar, pl.ds(0, ROWS), :]
            imag = sb[av, au, ar, pl.ds(ROWS, ROWS), :]
            less = real - imag
            more = real + imag
            base = ((n % 2) * SIDE + r) * (2 * Q * 8)
            for slot in range(2 * Q):
                i = idx[slot // Q, (a + blocks - slot % Q) & (blocks - 1)]
                k1 = fold(xs[i, 2] * imag)
                k2 = fold(xs[i, 0] * less)
                k3 = fold(xs[i, 1] * more)
                at = pl.ds(pl.multiple_of(base + slot * 8, 8), 8)
                ca[at, :] = k1 + k2
                cb[at, :] = k1 - k3

        @pl.when(n % 2 == 1)
        def _():
            lags = jnp.zeros((GROUP * 2 * Q, OUT), jnp.float32)
            for k in range(PERIOD // LANES):
                pick = pl.ds(k, GROUP * 2 * Q, stride=8)
                left = jnp.concatenate([ca[pick, :], cb[pick, :]], axis=1).astype(jnp.bfloat16)
                lags += jnp.dot(left, table[k], preferred_element_type=jnp.float32)
            first = (n // 2) * GROUP
            stage[pl.ds(first, GROUP)] = lags.astype(jnp.bfloat16).reshape(GROUP, 2 * Q, OUT)

            @pl.loop(0, GROUP)
            def _(member):
                turn = first + member
                av, au, ar = block_at(turn)

                @pl.when(turn > 0)
                def _():
                    remote(
                        stage.at[turn],
                        recv.at[row, band],
                        out_send,
                        out_recv,
                        (number(av, au, ar), side),
                    ).start()

    @pl.when(side == band)
    def _():
        pltpu.make_async_copy(stage.at[0], recv.at[row, band], out_recv).start()

    @pl.when(side != band)
    def _():
        copy = remote(stage.at[0], recv.at[row, band], twin_send, out_recv, twin)
        copy.start()
        copy.wait_send()

    for copy in pending:
        copy.wait_send()
    for n in range(1, 16):
        row_copy(n, PATH[n][0]).wait_send()
    pltpu.make_async_copy(
        stage.at[pl.ds(1, blocks - 1)], stage.at[pl.ds(1, blocks - 1)], out_send
    ).wait()
    pltpu.make_async_copy(recv, recv, out_recv).wait()


def unscramble(recv, out, near, wide, in_sem, out_sem):
    to = lax.broadcasted_iota(jnp.int32, (256, 256), 0)
    at = lax.broadcasted_iota(jnp.int32, (256, 256), 1)
    steps = [(s, g) for s in range(2) for g in range(4)]
    takes = []
    for n, (s, g) in enumerate(steps):
        block = pl.ds(8 * g, 8)
        take = pltpu.make_async_copy(recv.at[block, s], near.at[s, block], in_sem.at[n])
        take.start()
        takes.append(take)
    move = ((to % 16) * 16 + to // 16 == at).astype(jnp.bfloat16)
    gives = []
    for n, (s, g) in enumerate(steps):
        takes[n].wait()
        value = near[s, 8 * g : 8 * g + 8].reshape(256, OUT)
        value = jnp.dot(move, value, preferred_element_type=jnp.float32)
        wide[s, :, 16 * g : 16 * g + 16, :] = value.reshape(Q, 16, OUT)
        row = pl.ds(16 * g, 16)
        give = pltpu.make_async_copy(wide.at[s, :, row, :], out.at[s, :, row, :], out_sem.at[n])
        give.start()
        gives.append(give)
    for give in gives:
        give.wait()


def per_device(traces, sources, owner):
    stations = traces.shape[0]
    blocks = lax.axis_size("blk")
    tiles = traces.shape[2] // LANES
    x_in = traces.reshape(stations, 2, tiles, LANES).transpose(0, 2, 1, 3)
    x_in = x_in.reshape(stations, 2 * tiles, LANES)
    s_in = sources.reshape(2, 2, tiles, LANES).transpose(0, 2, 1, 3).reshape(2, 2 * tiles, LANES)
    table = jnp.asarray(lag_table())
    vmem = pl.BlockSpec(memory_space=pltpu.VMEM)
    recv = pl.pallas_call(
        correlate,
        out_shape=jax.ShapeDtypeStruct((blocks // 2, 2, 2 * Q, OUT), jnp.bfloat16),
        in_specs=[
            vmem,
            pl.BlockSpec(memory_space=pl.ANY),
            pl.BlockSpec(memory_space=pl.ANY),
            pl.BlockSpec(memory_space=pl.ANY),
        ],
        out_specs=pl.BlockSpec(memory_space=pl.ANY),
        scratch_shapes=[
            pltpu.VMEM((PERIOD // LANES, 2 * LANES, OUT), jnp.bfloat16),
            pltpu.VMEM((2, LANES), jnp.int32),
            pltpu.SMEM((2, LANES), jnp.int32),
            pltpu.VMEM((8, 2 * ROWS, LANES), jnp.float32),
            pltpu.VMEM((stations, 2 * ROWS, LANES), jnp.bfloat16),
            pltpu.VMEM((stations + 1, 3, ROWS, LANES), jnp.bfloat16),
            pltpu.VMEM((2 * ROWS, LANES), jnp.bfloat16),
            pltpu.VMEM((SIDE, SIDE, SIDE, 2 * ROWS, LANES), jnp.bfloat16),
            pltpu.VMEM((GROUP * 2 * Q * 8, LANES), jnp.float32),
            pltpu.VMEM((GROUP * 2 * Q * 8, LANES), jnp.float32),
            pltpu.VMEM((blocks, 2 * Q, OUT), jnp.bfloat16),
            pltpu.SemaphoreType.DMA((2,)),
            pltpu.SemaphoreType.DMA((2,)),
            pltpu.SemaphoreType.DMA((4,)),
            pltpu.SemaphoreType.DMA((18,)),
            pltpu.SemaphoreType.DMA((18,)),
            pltpu.SemaphoreType.DMA,
            pltpu.SemaphoreType.DMA,
            pltpu.SemaphoreType.DMA,
        ],
        compiler_params=pltpu.CompilerParams(
            has_side_effects=True, collective_id=0, vmem_limit_bytes=60 * 1024 * 1024
        ),
        name="correlate",
    )(owner.reshape(1, stations), x_in, s_in, table)
    return pl.pallas_call(
        unscramble,
        out_shape=jax.ShapeDtypeStruct((2, Q, 64, OUT), jnp.float32),
        in_specs=[pl.BlockSpec(memory_space=pl.ANY)],
        out_specs=pl.BlockSpec(memory_space=pl.ANY),
        scratch_shapes=[
            pltpu.VMEM((2, blocks // 2, 2 * Q, OUT), jnp.bfloat16),
            pltpu.VMEM((2, Q, 64, OUT), jnp.float32),
            pltpu.SemaphoreType.DMA((8,)),
            pltpu.SemaphoreType.DMA((8,)),
        ],
        compiler_params=pltpu.CompilerParams(vmem_limit_bytes=60 * 1024 * 1024),
        name="unscramble",
    )(recv)


def solution(mesh):
    placed = (P("blk", None, "band"), P("blk", None, "band"), P("blk", None))
    return jax.shard_map(
        per_device,
        mesh=mesh,
        in_specs=placed,
        out_specs=P("blk", None, "band", None),
        check_vma=False,
    )
```

```python
import math

import jax
import jax.numpy as jnp
import numpy as np
from jax import lax
from jax.experimental import pallas as pl
from jax.experimental.pallas import tpu as pltpu
from jax.sharding import PartitionSpec as P

BINS = 8192
DEC = 8
OUT = 256
EPS = 1e-06
Q = 16
PERIOD = BINS // DEC
LANES = 128
SIDE = 4
ROWS = BINS // LANES
GROUP = 8
PATH = (
    ((0, 0), None),
    ((1, 0), (1, 0)),
    ((3, 0), (3, 0)),
    ((0, 1), (0, 1)),
    ((0, 3), (0, 3)),
    ((1, 1), (1, 0)),
    ((3, 3), (3, 0)),
    ((0, 2), (0, 1)),
    ((1, 3), (0, 3)),
    ((2, 0), (1, 0)),
    ((3, 1), (3, 0)),
    ((1, 2), (0, 1)),
    ((2, 1), (1, 0)),
    ((2, 3), (3, 0)),
    ((2, 2), (1, 0)),
    ((3, 2), (3, 0)),
)
CODES = [
    np.uint32(sum((du + 4 * dv) << (4 * n) for n, ((du, dv), _) in enumerate(half))).astype(np.int32)
    for half in (PATH[:8], PATH[8:])
]
ROUNDS = {1: range(1, 5), 5: range(5, 9), 9: range(9, 12), 12: range(12, 14), 14: range(14, 16)}


def lag_table():
    bins = np.arange(PERIOD)[:, None]
    lags = np.arange(OUT)[None, :] - OUT // 2
    angle = 2.0 * np.pi * ((bins * lags) % PERIOD) / PERIOD
    shape = (PERIOD // LANES, LANES, OUT)
    both = [np.cos(angle).reshape(shape), np.sin(angle).reshape(shape)]
    return (np.concatenate(both, axis=1) / math.sqrt(BINS)).astype(jnp.bfloat16)


def whiten(block, wide):
    values = block.astype(jnp.float32)
    total = jnp.sum(jnp.sum(values * values, axis=0, keepdims=True), axis=1, keepdims=True)
    wide[...] = values * lax.rsqrt(total / (2 * BINS) + EPS)
    return [wide[pl.ds(part, ROWS, stride=2), :].astype(jnp.bfloat16) for part in range(2)]


def find_slots(owner, found):
    stations = owner.shape[1]
    shape = (stations, stations)
    j = lax.broadcasted_iota(jnp.int32, shape, 0)
    b = lax.broadcasted_iota(jnp.int32, shape, 1)
    named = jnp.sum(jnp.where(j == b, owner[...], 0), axis=1, keepdims=True)
    hits = named == b
    first = jnp.min(jnp.where(hits, j, stations), axis=0, keepdims=True)
    last = jnp.max(jnp.where(hits, j, -1), axis=0, keepdims=True)
    found[0:1, 0:stations] = first
    found[1:2, 0:stations] = jnp.where(last > first, last, stations)


def fold(products):
    pairs = (products[0:16] + products[16:32]) + (products[32:48] + products[48:64])
    pairs = pairs.astype(jnp.float32)
    return pairs[0:8] + pairs[8:16]


def correlate(
    owner,
    x_in,
    s_in,
    table_in,
    recv,
    table,
    found,
    idx,
    wide,
    raw,
    xs,
    source,
    sb,
    ca,
    cb,
    stage,
    pair_send,
    pair_recv,
    local_sem,
    ring_send,
    ring_recv,
    out_send,
    out_recv,
    twin_send,
):
    blk = lax.axis_index("blk")
    band = lax.axis_index("band")
    blocks = SIDE**3
    stations = x_in.shape[0]
    twin = (blk, 1 - band)
    size_u = jnp.where(band == 0, SIDE, 1)
    size_r = jnp.where(band == 0, 1, SIDE)
    px, py, pv = blk % SIDE, (blk // SIDE) % SIDE, blk // (SIDE * SIDE)
    pr = jnp.where(band == 0, px, py)
    pu = jnp.where(band == 0, py, px)

    def number(v, u, r):
        return v * (SIDE * SIDE) + u * size_u + r * size_r

    def device(du, dv, dr):
        return (number((pv + dv) & 3, (pu + du) & 3, (pr + dr) & 3), band)

    def remote(src, dst, send, recv_sem, target):
        return pltpu.make_async_remote_copy(
            src_ref=src,
            dst_ref=dst,
            send_sem=send,
            recv_sem=recv_sem,
            device_id=target,
            device_id_type=pl.DeviceIdType.MESH,
        )

    barrier = pltpu.get_barrier_semaphore()
    greeted = [twin]
    for step in (1, 2, 3):
        greeted += [device(step, 0, 0), device(0, step, 0), device(0, 0, step)]
    greeted = [g for n, g in enumerate(greeted) if n not in (4, 5)]
    for target in greeted:
        pl.semaphore_signal(barrier, inc=1, device_id=target, device_id_type=pl.DeviceIdType.MESH)

    mine = pl.ds(pl.multiple_of(band * ROWS, ROWS), ROWS)
    source_keep = pltpu.make_async_copy(s_in.at[band], source.at[mine, :], local_sem.at[0])
    source_keep.start()
    station_keep = pltpu.make_async_copy(x_in, raw.at[:, mine, :], local_sem.at[1])
    station_keep.start()
    table_copy = pltpu.make_async_copy(table_in, table, local_sem.at[3])
    table_copy.start()
    find_slots(owner, found)
    index_copy = pltpu.make_async_copy(found, idx, local_sem.at[2])
    index_copy.start()
    xs[stations] = jnp.zeros(xs.shape[1:], xs.dtype)
    pl.semaphore_wait(barrier, len(greeted))

    source_out = remote(
        s_in.at[1 - band], source.at[mine, :], pair_send.at[0], pair_recv.at[0], twin
    )
    source_out.start()
    station_out = remote(x_in, raw.at[:, mine, :], pair_send.at[1], pair_recv.at[1], twin)
    station_out.start()
    source_keep.wait()
    source_out.wait_recv()
    own = whiten(source[...], wide.at[0])
    for part in range(2):
        sb[pv, pu, pr, part * ROWS : (part + 1) * ROWS] = own[part]
    pending = [source_out, station_out]

    def r_copy(step, at):
        block = sb.at[pv, pu, at]
        return remote(
            block, block, ring_send.at[15 + step - 1], ring_recv.at[15 + step - 1], device(0, 0, step)
        )

    for step in (1, 3, 2):
        copy = r_copy(step, pr)
        copy.start()
        pending.append(copy)
    for step in (1, 3, 2):
        r_copy(step, (pr + 4 - step) & 3).wait_recv()

    def row_copy(n, place):
        row = sb.at[(pv + 4 - place[1]) & 3, (pu + 4 - place[0]) & 3]
        step = PATH[n][1]
        return remote(
            row, row, ring_send.at[n - 1], ring_recv.at[n - 1], device(step[0], step[1], 0)
        )

    def pass_on(n):
        place = PATH[n][0]
        for child in range(1, 16):
            there, step = PATH[child]
            if ((there[0] - step[0]) % 4, (there[1] - step[1]) % 4) == place:
                row_copy(child, place).start()

    pass_on(0)
    index_copy.wait()
    table_copy.wait()

    station_keep.wait()
    station_out.wait_recv()

    @pl.loop(0, stations // 8)
    def _(group):
        for member in range(8):
            i = group * 8 + member
            real, imag = whiten(raw[i], wide.at[member])
            xs[i, 0] = real
            xs[i, 1] = imag
            xs[i, 2] = real + imag

    side = blk // (blocks // 2)
    row = blk % (blocks // 2)

    def row_at(n):
        code = jnp.where(n < 8, CODES[0], CODES[1]) >> ((n & 7) * 4)
        return (pv + 4 - ((code >> 2) & 3)) & 3, (pu + 4 - (code & 3)) & 3

    def send_lags(n, r):
        v, u = row_at(n)
        remote(
            stage.at[n * SIDE + r],
            recv.at[row, band],
            out_send,
            out_recv,
            (number(v, u, (pr + r) & 3), side),
        ).start()

    def spectra(n, v, u, r):
        ar = (pr + r) & 3
        a = number(v, u, ar)
        real = sb[v, u, ar, pl.ds(0, ROWS), :]
        imag = sb[v, u, ar, pl.ds(ROWS, ROWS), :]
        less = real - imag
        more = real + imag
        base = ((n % 2) * SIDE + r) * (2 * Q * 8)
        for slot in range(2 * Q):
            i = idx[slot // Q, (a + blocks - slot % Q) & (blocks - 1)]
            k1 = fold(xs[i, 2] * imag)
            k2 = fold(xs[i, 0] * less)
            k3 = fold(xs[i, 1] * more)
            at = pl.ds(pl.multiple_of(base + slot * 8, 8), 8)
            ca[at, :] = k1 + k2
            cb[at, :] = k1 - k3

    @pl.loop(0, blocks // SIDE)
    def _(n):
        for when, arrivals in ROUNDS.items():

            @pl.when(n == when)
            def _():
                for k in arrivals:
                    row_copy(k, PATH[k][0]).wait_recv()
                    pass_on(k)

        @pl.when(n > 2)
        def _():
            send_lags(n - 2, 0)

        @pl.when(n > 1)
        def _():
            for r in range(1, SIDE):
                send_lags(n - 2, r)

        v, u = row_at(n)

        @pl.loop(0, SIDE)
        def _(r):
            spectra(n, v, u, r)

        @pl.when(n % 2 == 1)
        def _():
            total = jnp.zeros((GROUP * 2 * Q, OUT), jnp.float32)
            for k in range(PERIOD // LANES):
                pick = pl.ds(k, GROUP * 2 * Q, stride=8)
                left = jnp.concatenate([ca[pick, :], cb[pick, :]], axis=1).astype(jnp.bfloat16)
                total += jnp.dot(left, table[k], preferred_element_type=jnp.float32)
            first = (n // 2) * GROUP
            stage[pl.ds(first, GROUP)] = total.astype(jnp.bfloat16).reshape(GROUP, 2 * Q, OUT)

    for n in (blocks // SIDE - 2, blocks // SIDE - 1):
        for r in range(SIDE):
            send_lags(n, r)

    @pl.when(side == band)
    def _():
        pltpu.make_async_copy(stage.at[0], recv.at[row, band], out_recv).start()

    @pl.when(side != band)
    def _():
        copy = remote(stage.at[0], recv.at[row, band], twin_send, out_recv, twin)
        copy.start()
        copy.wait_send()

    for copy in pending:
        copy.wait_send()
    for n in range(1, 16):
        row_copy(n, PATH[n][0]).wait_send()
    pltpu.make_async_copy(
        stage.at[pl.ds(1, blocks - 1)], stage.at[pl.ds(1, blocks - 1)], out_send
    ).wait()
    pltpu.make_async_copy(recv, recv, out_recv).wait()


def unscramble(recv, out, near, wide, in_sem, out_sem):
    to = lax.broadcasted_iota(jnp.int32, (256, 256), 0)
    at = lax.broadcasted_iota(jnp.int32, (256, 256), 1)
    steps = [(s, g) for s in range(2) for g in range(4)]
    takes = []
    for n, (s, g) in enumerate(steps):
        block = pl.ds(8 * g, 8)
        take = pltpu.make_async_copy(recv.at[block, s], near.at[s, block], in_sem.at[n])
        take.start()
        takes.append(take)
    move = ((to % 16) * 16 + to // 16 == at).astype(jnp.bfloat16)
    gives = []
    for n, (s, g) in enumerate(steps):
        takes[n].wait()
        value = near[s, 8 * g : 8 * g + 8].reshape(256, OUT)
        value = jnp.dot(move, value, preferred_element_type=jnp.float32)
        wide[s, :, 16 * g : 16 * g + 16, :] = value.reshape(Q, 16, OUT)
        row = pl.ds(16 * g, 16)
        give = pltpu.make_async_copy(wide.at[s, :, row, :], out.at[s, :, row, :], out_sem.at[n])
        give.start()
        gives.append(give)
    for give in gives:
        give.wait()


def per_device(traces, sources, owner):
    stations = traces.shape[0]
    blocks = lax.axis_size("blk")
    tiles = traces.shape[2] // LANES
    x_in = traces.reshape(stations, 2, tiles, LANES).transpose(0, 2, 1, 3)
    x_in = x_in.reshape(stations, 2 * tiles, LANES)
    s_in = sources.reshape(2, 2, tiles, LANES).transpose(0, 2, 1, 3).reshape(2, 2 * tiles, LANES)
    table = jnp.asarray(lag_table())
    vmem = pl.BlockSpec(memory_space=pltpu.VMEM)
    recv = pl.pallas_call(
        correlate,
        out_shape=jax.ShapeDtypeStruct((blocks // 2, 2, 2 * Q, OUT), jnp.bfloat16),
        in_specs=[
            vmem,
            pl.BlockSpec(memory_space=pl.ANY),
            pl.BlockSpec(memory_space=pl.ANY),
            pl.BlockSpec(memory_space=pl.ANY),
        ],
        out_specs=pl.BlockSpec(memory_space=pl.ANY),
        scratch_shapes=[
            pltpu.VMEM((PERIOD // LANES, 2 * LANES, OUT), jnp.bfloat16),
            pltpu.VMEM((2, LANES), jnp.int32),
            pltpu.SMEM((2, LANES), jnp.int32),
            pltpu.VMEM((8, 2 * ROWS, LANES), jnp.float32),
            pltpu.VMEM((stations, 2 * ROWS, LANES), jnp.bfloat16),
            pltpu.VMEM((stations + 1, 3, ROWS, LANES), jnp.bfloat16),
            pltpu.VMEM((2 * ROWS, LANES), jnp.bfloat16),
            pltpu.VMEM((SIDE, SIDE, SIDE, 2 * ROWS, LANES), jnp.bfloat16),
            pltpu.VMEM((GROUP * 2 * Q * 8, LANES), jnp.float32),
            pltpu.VMEM((GROUP * 2 * Q * 8, LANES), jnp.float32),
            pltpu.VMEM((blocks, 2 * Q, OUT), jnp.bfloat16),
            pltpu.SemaphoreType.DMA((2,)),
            pltpu.SemaphoreType.DMA((2,)),
            pltpu.SemaphoreType.DMA((4,)),
            pltpu.SemaphoreType.DMA((18,)),
            pltpu.SemaphoreType.DMA((18,)),
            pltpu.SemaphoreType.DMA,
            pltpu.SemaphoreType.DMA,
            pltpu.SemaphoreType.DMA,
        ],
        compiler_params=pltpu.CompilerParams(
            has_side_effects=True, collective_id=0, vmem_limit_bytes=60 * 1024 * 1024
        ),
        name="correlate",
    )(owner.reshape(1, stations), x_in, s_in, table)
    return pl.pallas_call(
        unscramble,
        out_shape=jax.ShapeDtypeStruct((2, Q, 64, OUT), jnp.float32),
        in_specs=[pl.BlockSpec(memory_space=pl.ANY)],
        out_specs=pl.BlockSpec(memory_space=pl.ANY),
        scratch_shapes=[
            pltpu.VMEM((2, blocks // 2, 2 * Q, OUT), jnp.bfloat16),
            pltpu.VMEM((2, Q, 64, OUT), jnp.float32),
            pltpu.SemaphoreType.DMA((8,)),
            pltpu.SemaphoreType.DMA((8,)),
        ],
        compiler_params=pltpu.CompilerParams(vmem_limit_bytes=60 * 1024 * 1024),
        name="unscramble",
    )(recv)


def solution(mesh):
    placed = (P("blk", None, "band"), P("blk", None, "band"), P("blk", None))
    return jax.shard_map(
        per_device,
        mesh=mesh,
        in_specs=placed,
        out_specs=P("blk", None, "band", None),
        check_vma=False,
    )
```

```python
import math

import jax
import jax.numpy as jnp
import numpy as np
from jax import lax
from jax.experimental import pallas as pl
from jax.experimental.pallas import tpu as pltpu
from jax.sharding import PartitionSpec as P

BINS = 8192
DEC = 8
OUT = 256
EPS = 1e-06
Q = 16
PERIOD = BINS // DEC
LANES = 128
SIDE = 4
ROWS = BINS // LANES
GROUP = 8
PATH = (
    ((0, 0), None),
    ((1, 0), (1, 0)),
    ((3, 0), (3, 0)),
    ((0, 1), (0, 1)),
    ((0, 3), (0, 3)),
    ((1, 1), (1, 0)),
    ((3, 3), (3, 0)),
    ((0, 2), (0, 1)),
    ((1, 3), (0, 3)),
    ((2, 0), (1, 0)),
    ((3, 1), (3, 0)),
    ((1, 2), (0, 1)),
    ((2, 1), (1, 0)),
    ((2, 3), (3, 0)),
    ((2, 2), (1, 0)),
    ((3, 2), (3, 0)),
)
WAVES = ((0,), (1, 2, 3, 4), (5, 6, 7, 8), (9, 10, 11), (12, 13), (14, 15))
ORDER = [(k, part) for wave in WAVES for part in (0, 1) for k in wave]


def word(values, bits):
    return np.uint32(sum(int(v) << (bits * n) for n, v in enumerate(values))).astype(np.int32)


CODES = [
    word([PATH[k][0][0] + 4 * PATH[k][0][1] for k, _ in ORDER[n : n + 8]], 4) for n in (0, 8, 16, 24)
]
HALVES = word([part for _, part in ORDER], 1)
ROUNDS = {2: (1, 0), 6: (1, 1), 10: (2, 0), 14: (2, 1), 18: (3, 0), 21: (3, 1), 24: (4, 0), 26: (4, 1), 28: (5, 0), 30: (5, 1)}
TAKES = sum(1 << when for when in ROUNDS)


def lag_table():
    bins = np.arange(PERIOD)[:, None]
    lags = np.arange(OUT)[None, :] - OUT // 2
    angle = 2.0 * np.pi * ((bins * lags) % PERIOD) / PERIOD
    shape = (PERIOD // LANES, LANES, OUT)
    both = [np.cos(angle).reshape(shape), np.sin(angle).reshape(shape)]
    return (np.concatenate(both, axis=1) / math.sqrt(BINS)).astype(jnp.bfloat16)


def whiten(block, wide):
    values = block.astype(jnp.float32)
    total = jnp.sum(jnp.sum(values * values, axis=0, keepdims=True), axis=1, keepdims=True)
    wide[...] = values * lax.rsqrt(total / (2 * BINS) + EPS)
    return [wide[pl.ds(part, ROWS, stride=2), :].astype(jnp.bfloat16) for part in range(2)]


def find_slots(owner, found):
    stations = owner.shape[1]
    shape = (stations, stations)
    j = lax.broadcasted_iota(jnp.int32, shape, 0)
    b = lax.broadcasted_iota(jnp.int32, shape, 1)
    named = jnp.sum(jnp.where(j == b, owner[...], 0), axis=1, keepdims=True)
    hits = named == b
    first = jnp.min(jnp.where(hits, j, stations), axis=0, keepdims=True)
    last = jnp.max(jnp.where(hits, j, -1), axis=0, keepdims=True)
    found[0:1, 0:stations] = first
    found[1:2, 0:stations] = jnp.where(last > first, last, stations)


def fold(products):
    pairs = (products[0:16] + products[16:32]) + (products[32:48] + products[48:64])
    pairs = pairs.astype(jnp.float32)
    return pairs[0:8] + pairs[8:16]


def correlate(
    owner,
    x_in,
    s_in,
    table_in,
    recv,
    table,
    found,
    idx,
    wide,
    raw,
    xs,
    source,
    sb,
    ca,
    cb,
    stage,
    pair_send,
    pair_recv,
    local_sem,
    ring_send,
    ring_recv,
    out_send,
    out_recv,
    twin_send,
):
    blk = lax.axis_index("blk")
    band = lax.axis_index("band")
    blocks = SIDE**3
    stations = x_in.shape[0]
    twin = (blk, 1 - band)
    size_u = jnp.where(band == 0, SIDE, 1)
    size_r = jnp.where(band == 0, 1, SIDE)
    px, py, pv = blk % SIDE, (blk // SIDE) % SIDE, blk // (SIDE * SIDE)
    pr = jnp.where(band == 0, px, py)
    pu = jnp.where(band == 0, py, px)

    def number(v, u, r):
        return v * (SIDE * SIDE) + u * size_u + r * size_r

    def device(du, dv, dr):
        return (number((pv + dv) & 3, (pu + du) & 3, (pr + dr) & 3), band)

    def remote(src, dst, send, recv_sem, target):
        return pltpu.make_async_remote_copy(
            src_ref=src,
            dst_ref=dst,
            send_sem=send,
            recv_sem=recv_sem,
            device_id=target,
            device_id_type=pl.DeviceIdType.MESH,
        )

    barrier = pltpu.get_barrier_semaphore()
    greeted = [twin]
    for step in (1, 2, 3):
        greeted += [device(step, 0, 0), device(0, step, 0), device(0, 0, step)]
    greeted = [g for n, g in enumerate(greeted) if n not in (4, 5)]
    for target in greeted:
        pl.semaphore_signal(barrier, inc=1, device_id=target, device_id_type=pl.DeviceIdType.MESH)

    mine = pl.ds(pl.multiple_of(band * ROWS, ROWS), ROWS)
    source_keep = pltpu.make_async_copy(s_in.at[band], source.at[mine, :], local_sem.at[0])
    source_keep.start()
    station_keep = pltpu.make_async_copy(x_in, raw.at[:, mine, :], local_sem.at[1])
    station_keep.start()
    table_copy = pltpu.make_async_copy(table_in, table, local_sem.at[3])
    table_copy.start()
    find_slots(owner, found)
    index_copy = pltpu.make_async_copy(found, idx, local_sem.at[2])
    index_copy.start()
    xs[stations] = jnp.zeros(xs.shape[1:], xs.dtype)
    pl.semaphore_wait(barrier, len(greeted))

    source_out = remote(
        s_in.at[1 - band], source.at[mine, :], pair_send.at[0], pair_recv.at[0], twin
    )
    source_out.start()
    station_out = remote(x_in, raw.at[:, mine, :], pair_send.at[1], pair_recv.at[1], twin)
    station_out.start()
    source_keep.wait()
    source_out.wait_recv()
    own = whiten(source[...], wide.at[0])
    for part in range(2):
        sb[pv, pu, pr, part * ROWS : (part + 1) * ROWS] = own[part]
    pending = [source_out, station_out]

    def r_copy(step, at):
        block = sb.at[pv, pu, at]
        return remote(
            block, block, ring_send.at[step - 1], ring_recv.at[step - 1], device(0, 0, step)
        )

    for step in (1, 3, 2):
        copy = r_copy(step, pr)
        copy.start()
        pending.append(copy)
    for step in (1, 3, 2):
        r_copy(step, (pr + 4 - step) & 3).wait_recv()

    def row_copy(n, part, place):
        halves = pl.ds(part * 2, 2)
        row = sb.at[(pv + 4 - place[1]) & 3, (pu + 4 - place[0]) & 3, halves]
        step = PATH[n][1]
        spot = 2 * n + part + 1
        return remote(row, row, ring_send.at[spot], ring_recv.at[spot], device(step[0], step[1], 0))

    def pass_on(n, part):
        place = PATH[n][0]
        for child in range(1, 16):
            there, step = PATH[child]
            if ((there[0] - step[0]) % 4, (there[1] - step[1]) % 4) == place:
                row_copy(child, part, place).start()

    for part in (0, 1):
        pass_on(0, part)
    index_copy.wait()
    table_copy.wait()

    station_keep.wait()
    station_out.wait_recv()

    @pl.loop(0, stations // 8)
    def _(group):
        for member in range(8):
            i = group * 8 + member
            real, imag = whiten(raw[i], wide.at[member])
            xs[i, 0] = real
            xs[i, 1] = imag
            xs[i, 2] = real + imag

    side = blk // (blocks // 2)
    row = blk % (blocks // 2)

    def half_row(n):
        code = jnp.where(n < 8, CODES[0], CODES[1])
        code = jnp.where(n < 16, code, jnp.where(n < 24, CODES[2], CODES[3])) >> ((n & 7) * 4)
        return (pv + 4 - ((code >> 2) & 3)) & 3, (pu + 4 - (code & 3)) & 3, ((HALVES >> n) & 1) * 2

    def send_lags(n, own_row):
        v, u, first = half_row(n)
        for j in range(2):

            def send():
                remote(
                    stage.at[n * 2 + j],
                    recv.at[row, band],
                    out_send,
                    out_recv,
                    (number(v, u, first + j), side),
                ).start()

            if own_row:
                pl.when(first + j != pr)(send)
            else:
                send()

    def spectra(n, v, u, r, j):
        a = number(v, u, r)
        real = sb[v, u, r, pl.ds(0, ROWS), :]
        imag = sb[v, u, r, pl.ds(ROWS, ROWS), :]
        less = real - imag
        more = real + imag
        base = ((n % 4) * 2 + j) * (2 * Q * 8)
        for slot in range(2 * Q):
            i = idx[slot // Q, (a + blocks - slot % Q) & (blocks - 1)]
            k1 = fold(xs[i, 2] * imag)
            k2 = fold(xs[i, 0] * less)
            k3 = fold(xs[i, 1] * more)
            at = pl.ds(pl.multiple_of(base + slot * 8, 8), 8)
            ca[at, :] = k1 + k2
            cb[at, :] = k1 - k3

    steps = blocks // 2

    @pl.loop(0, steps)
    def _(n):
        @pl.when(((TAKES >> n) & 1) == 1)
        def _():
            for when, (wave, part) in ROUNDS.items():

                @pl.when(n == when)
                def _():
                    for k in WAVES[wave]:
                        row_copy(k, part, PATH[k][0]).wait_recv()
                        pass_on(k, part)

        @pl.when(n > 5)
        def _():
            send_lags(n - 4, False)

        @pl.when((n == 4) | (n == 5))
        def _():
            send_lags(n - 4, True)

        v, u, first = half_row(n)

        @pl.loop(0, 2)
        def _(j):
            spectra(n, v, u, first + j, j)

        @pl.when(n % 4 == 3)
        def _():
            total = jnp.zeros((GROUP * 2 * Q, OUT), jnp.float32)
            for k in range(PERIOD // LANES):
                pick = pl.ds(k, GROUP * 2 * Q, stride=8)
                left = jnp.concatenate([ca[pick, :], cb[pick, :]], axis=1).astype(jnp.bfloat16)
                total += jnp.dot(left, table[k], preferred_element_type=jnp.float32)
            at = (n // 4) * GROUP
            stage[pl.ds(at, GROUP)] = total.astype(jnp.bfloat16).reshape(GROUP, 2 * Q, OUT)

    for n in range(steps - 4, steps):
        send_lags(n, False)

    @pl.when(side == band)
    def _():
        pltpu.make_async_copy(stage.at[pr], recv.at[row, band], out_recv).start()

    @pl.when(side != band)
    def _():
        copy = remote(stage.at[pr], recv.at[row, band], twin_send, out_recv, twin)
        copy.start()
        copy.wait_send()

    for copy in pending:
        copy.wait_send()
    for n in range(1, 16):
        for part in (0, 1):
            row_copy(n, part, PATH[n][0]).wait_send()
    pltpu.make_async_copy(
        stage.at[pl.ds(1, blocks - 1)], stage.at[pl.ds(1, blocks - 1)], out_send
    ).wait()
    pltpu.make_async_copy(recv, recv, out_recv).wait()


def unscramble(recv, out, near, wide, in_sem, out_sem):
    to = lax.broadcasted_iota(jnp.int32, (256, 256), 0)
    at = lax.broadcasted_iota(jnp.int32, (256, 256), 1)
    steps = [(s, g) for s in range(2) for g in range(4)]
    takes = []
    for n, (s, g) in enumerate(steps):
        block = pl.ds(8 * g, 8)
        take = pltpu.make_async_copy(recv.at[block, s], near.at[s, block], in_sem.at[n])
        take.start()
        takes.append(take)
    move = ((to % 16) * 16 + to // 16 == at).astype(jnp.bfloat16)
    gives = []
    for n, (s, g) in enumerate(steps):
        takes[n].wait()
        value = near[s, 8 * g : 8 * g + 8].reshape(256, OUT)
        value = jnp.dot(move, value, preferred_element_type=jnp.float32)
        wide[s, :, 16 * g : 16 * g + 16, :] = value.reshape(Q, 16, OUT)
        row = pl.ds(16 * g, 16)
        give = pltpu.make_async_copy(wide.at[s, :, row, :], out.at[s, :, row, :], out_sem.at[n])
        give.start()
        gives.append(give)
    for give in gives:
        give.wait()


def per_device(traces, sources, owner):
    stations = traces.shape[0]
    blocks = lax.axis_size("blk")
    tiles = traces.shape[2] // LANES
    x_in = traces.reshape(stations, 2, tiles, LANES).transpose(0, 2, 1, 3)
    x_in = x_in.reshape(stations, 2 * tiles, LANES)
    s_in = sources.reshape(2, 2, tiles, LANES).transpose(0, 2, 1, 3).reshape(2, 2 * tiles, LANES)
    table = jnp.asarray(lag_table())
    vmem = pl.BlockSpec(memory_space=pltpu.VMEM)
    recv = pl.pallas_call(
        correlate,
        out_shape=jax.ShapeDtypeStruct((blocks // 2, 2, 2 * Q, OUT), jnp.bfloat16),
        in_specs=[
            vmem,
            pl.BlockSpec(memory_space=pl.ANY),
            pl.BlockSpec(memory_space=pl.ANY),
            pl.BlockSpec(memory_space=pl.ANY),
        ],
        out_specs=pl.BlockSpec(memory_space=pl.ANY),
        scratch_shapes=[
            pltpu.VMEM((PERIOD // LANES, 2 * LANES, OUT), jnp.bfloat16),
            pltpu.VMEM((2, LANES), jnp.int32),
            pltpu.SMEM((2, LANES), jnp.int32),
            pltpu.VMEM((8, 2 * ROWS, LANES), jnp.float32),
            pltpu.VMEM((stations, 2 * ROWS, LANES), jnp.bfloat16),
            pltpu.VMEM((stations + 1, 3, ROWS, LANES), jnp.bfloat16),
            pltpu.VMEM((2 * ROWS, LANES), jnp.bfloat16),
            pltpu.VMEM((SIDE, SIDE, SIDE, 2 * ROWS, LANES), jnp.bfloat16),
            pltpu.VMEM((GROUP * 2 * Q * 8, LANES), jnp.float32),
            pltpu.VMEM((GROUP * 2 * Q * 8, LANES), jnp.float32),
            pltpu.VMEM((blocks, 2 * Q, OUT), jnp.bfloat16),
            pltpu.SemaphoreType.DMA((2,)),
            pltpu.SemaphoreType.DMA((2,)),
            pltpu.SemaphoreType.DMA((4,)),
            pltpu.SemaphoreType.DMA((33,)),
            pltpu.SemaphoreType.DMA((33,)),
            pltpu.SemaphoreType.DMA,
            pltpu.SemaphoreType.DMA,
            pltpu.SemaphoreType.DMA,
        ],
        compiler_params=pltpu.CompilerParams(
            has_side_effects=True, collective_id=0, vmem_limit_bytes=60 * 1024 * 1024
        ),
        name="correlate",
    )(owner.reshape(1, stations), x_in, s_in, table)
    return pl.pallas_call(
        unscramble,
        out_shape=jax.ShapeDtypeStruct((2, Q, 64, OUT), jnp.float32),
        in_specs=[pl.BlockSpec(memory_space=pl.ANY)],
        out_specs=pl.BlockSpec(memory_space=pl.ANY),
        scratch_shapes=[
            pltpu.VMEM((2, blocks // 2, 2 * Q, OUT), jnp.bfloat16),
            pltpu.VMEM((2, Q, 64, OUT), jnp.float32),
            pltpu.SemaphoreType.DMA((8,)),
            pltpu.SemaphoreType.DMA((8,)),
        ],
        compiler_params=pltpu.CompilerParams(vmem_limit_bytes=60 * 1024 * 1024),
        name="unscramble",
    )(recv)


def solution(mesh):
    placed = (P("blk", None, "band"), P("blk", None, "band"), P("blk", None))
    return jax.shard_map(
        per_device,
        mesh=mesh,
        in_specs=placed,
        out_specs=P("blk", None, "band", None),
        check_vma=False,
    )
```

```python
import math

import jax
import jax.numpy as jnp
import numpy as np
from jax import lax
from jax.experimental import pallas as pl
from jax.experimental.pallas import tpu as pltpu
from jax.sharding import PartitionSpec as P

BINS = 8192
DEC = 8
OUT = 256
EPS = 1e-06
Q = 16
PERIOD = BINS // DEC
LANES = 128
SIDE = 4
ROWS = BINS // LANES
GROUP = 8
PATH = (
    ((0, 0), None),
    ((1, 0), (1, 0)),
    ((3, 0), (3, 0)),
    ((0, 1), (0, 1)),
    ((0, 3), (0, 3)),
    ((1, 1), (1, 0)),
    ((3, 3), (3, 0)),
    ((0, 2), (0, 1)),
    ((1, 3), (0, 3)),
    ((2, 0), (1, 0)),
    ((3, 1), (3, 0)),
    ((1, 2), (0, 1)),
    ((2, 1), (1, 0)),
    ((2, 3), (3, 0)),
    ((2, 2), (1, 0)),
    ((3, 2), (3, 0)),
)
WAVES = ((0,), (1, 2, 3, 4), (5, 6, 7, 8), (9, 10, 11), (12, 13), (14, 15))
ORDER = [(k, part) for wave in WAVES for part in (0, 1) for k in wave]


def word(values, bits):
    return np.uint32(sum(int(v) << (bits * n) for n, v in enumerate(values))).astype(np.int32)


CODES = [
    word([PATH[k][0][0] + 4 * PATH[k][0][1] for k, _ in ORDER[n : n + 8]], 4) for n in (0, 8, 16, 24)
]
HALVES = word([part for _, part in ORDER], 1)
ROUNDS = {2: (1, 0), 6: (1, 1), 10: (2, 0), 14: (2, 1), 18: (3, 0), 21: (3, 1), 24: (4, 0), 26: (4, 1), 28: (5, 0), 30: (5, 1)}
TAKES = sum(1 << when for when in ROUNDS)


def lag_table():
    bins = np.arange(PERIOD)[:, None]
    lags = np.arange(OUT)[None, :] - OUT // 2
    angle = 2.0 * np.pi * ((bins * lags) % PERIOD) / PERIOD
    shape = (PERIOD // LANES, LANES, OUT)
    both = [np.cos(angle).reshape(shape), np.sin(angle).reshape(shape)]
    return (np.concatenate(both, axis=1) / math.sqrt(BINS)).astype(jnp.bfloat16)


def whiten(block, wide):
    values = block.astype(jnp.float32)
    total = jnp.sum(jnp.sum(values * values, axis=0, keepdims=True), axis=1, keepdims=True)
    wide[...] = values * lax.rsqrt(total / (2 * BINS) + EPS)
    return [wide[pl.ds(part, ROWS, stride=2), :].astype(jnp.bfloat16) for part in range(2)]


def find_slots(owner, found):
    stations = owner.shape[1]
    shape = (stations, stations)
    j = lax.broadcasted_iota(jnp.int32, shape, 0)
    b = lax.broadcasted_iota(jnp.int32, shape, 1)
    named = jnp.sum(jnp.where(j == b, owner[...], 0), axis=1, keepdims=True)
    hits = named == b
    first = jnp.min(jnp.where(hits, j, stations), axis=0, keepdims=True)
    last = jnp.max(jnp.where(hits, j, -1), axis=0, keepdims=True)
    found[0:1, 0:stations] = first
    found[1:2, 0:stations] = jnp.where(last > first, last, stations)


def fold(products):
    pairs = (products[0:16] + products[16:32]) + (products[32:48] + products[48:64])
    pairs = pairs.astype(jnp.float32)
    return pairs[0:8] + pairs[8:16]


def correlate(
    owner,
    x_in,
    s_in,
    table_in,
    recv,
    table,
    found,
    idx,
    wide,
    raw,
    xs,
    source,
    sb,
    ca,
    cb,
    stage,
    pair_send,
    pair_recv,
    local_sem,
    ring_send,
    ring_recv,
    out_send,
    out_recv,
    twin_send,
):
    blk = lax.axis_index("blk")
    band = lax.axis_index("band")
    blocks = SIDE**3
    stations = x_in.shape[0]
    twin = (blk, 1 - band)
    size_u = jnp.where(band == 0, SIDE, 1)
    size_r = jnp.where(band == 0, 1, SIDE)
    px, py, pv = blk % SIDE, (blk // SIDE) % SIDE, blk // (SIDE * SIDE)
    pr = jnp.where(band == 0, px, py)
    pu = jnp.where(band == 0, py, px)

    def number(v, u, r):
        return v * (SIDE * SIDE) + u * size_u + r * size_r

    def device(du, dv, dr):
        return (number((pv + dv) & 3, (pu + du) & 3, (pr + dr) & 3), band)

    def remote(src, dst, send, recv_sem, target):
        return pltpu.make_async_remote_copy(
            src_ref=src,
            dst_ref=dst,
            send_sem=send,
            recv_sem=recv_sem,
            device_id=target,
            device_id_type=pl.DeviceIdType.MESH,
        )

    barrier = pltpu.get_barrier_semaphore()
    greeted = [twin]
    for step in (1, 2, 3):
        greeted += [device(step, 0, 0), device(0, step, 0), device(0, 0, step)]
    greeted = [g for n, g in enumerate(greeted) if n not in (4, 5)]
    for target in greeted:
        pl.semaphore_signal(barrier, inc=1, device_id=target, device_id_type=pl.DeviceIdType.MESH)

    mine = pl.ds(pl.multiple_of(band * ROWS, ROWS), ROWS)
    source_keep = pltpu.make_async_copy(s_in.at[band], source.at[mine, :], local_sem.at[0])
    source_keep.start()
    station_keep = pltpu.make_async_copy(x_in, raw.at[:, mine, :], local_sem.at[1])
    station_keep.start()
    table_copy = pltpu.make_async_copy(table_in, table, local_sem.at[3])
    table_copy.start()
    find_slots(owner, found)
    index_copy = pltpu.make_async_copy(found, idx, local_sem.at[2])
    index_copy.start()
    xs[stations] = jnp.zeros(xs.shape[1:], xs.dtype)
    pl.semaphore_wait(barrier, len(greeted))

    source_out = remote(
        s_in.at[1 - band], source.at[mine, :], pair_send.at[0], pair_recv.at[0], twin
    )
    source_out.start()
    station_out = remote(x_in, raw.at[:, mine, :], pair_send.at[1], pair_recv.at[1], twin)
    station_out.start()
    source_keep.wait()
    source_out.wait_recv()
    own = whiten(source[...], wide.at[0])
    for part in range(2):
        sb[pv, pu, pr, part * ROWS : (part + 1) * ROWS] = own[part]
    pending = [source_out, station_out]

    def r_copy(step, at):
        block = sb.at[pv, pu, at]
        return remote(
            block, block, ring_send.at[step - 1], ring_recv.at[step - 1], device(0, 0, step)
        )

    for step in (1, 3, 2):
        copy = r_copy(step, pr)
        copy.start()
        pending.append(copy)
    for step in (1, 3, 2):
        r_copy(step, (pr + 4 - step) & 3).wait_recv()

    def row_copy(n, part, place):
        halves = pl.ds(part * 2, 2)
        row = sb.at[(pv + 4 - place[1]) & 3, (pu + 4 - place[0]) & 3, halves]
        step = PATH[n][1]
        spot = 2 * n + part + 1
        return remote(row, row, ring_send.at[spot], ring_recv.at[spot], device(step[0], step[1], 0))

    def pass_on(n, part):
        place = PATH[n][0]
        for child in range(1, 16):
            there, step = PATH[child]
            if ((there[0] - step[0]) % 4, (there[1] - step[1]) % 4) == place:
                row_copy(child, part, place).start()

    for part in (0, 1):
        pass_on(0, part)
    index_copy.wait()
    table_copy.wait()

    station_keep.wait()
    station_out.wait_recv()

    @pl.loop(0, stations // 8)
    def _(group):
        for member in range(8):
            i = group * 8 + member
            real, imag = whiten(raw[i], wide.at[member])
            xs[i, 0] = real
            xs[i, 1] = imag
            xs[i, 2] = real + imag

    side = blk // (blocks // 2)
    row = blk % (blocks // 2)

    def half_row(n):
        code = jnp.where(n < 8, CODES[0], CODES[1])
        code = jnp.where(n < 16, code, jnp.where(n < 24, CODES[2], CODES[3])) >> ((n & 7) * 4)
        return (pv + 4 - ((code >> 2) & 3)) & 3, (pu + 4 - (code & 3)) & 3, ((HALVES >> n) & 1) * 2

    def send_lags(n, own_row):
        v, u, first = half_row(n)
        for j in range(2):

            def send():
                remote(
                    stage.at[n * 2 + j],
                    recv.at[row, band],
                    out_send,
                    out_recv,
                    (number(v, u, first + j), side),
                ).start()

            if own_row:
                pl.when(first + j != pr)(send)
            else:
                send()

    def spectra(n, v, u, r, j):
        a = number(v, u, r)
        real = sb[v, u, r, pl.ds(0, ROWS), :]
        imag = sb[v, u, r, pl.ds(ROWS, ROWS), :]
        less = real - imag
        more = real + imag
        base = ((n % 4) * 2 + j) * (2 * Q * 8)
        for slot in range(2 * Q):
            i = idx[slot // Q, (a + blocks - slot % Q) & (blocks - 1)]
            k1 = fold(xs[i, 2] * imag)
            k2 = fold(xs[i, 0] * less)
            k3 = fold(xs[i, 1] * more)
            at = pl.ds(pl.multiple_of(base + slot * 8, 8), 8)
            ca[at, :] = k1 + k2
            cb[at, :] = k1 - k3

    steps = blocks // 2

    @pl.loop(0, steps)
    def _(n):
        @pl.when(((TAKES >> n) & 1) == 1)
        def _():
            for when, (wave, part) in ROUNDS.items():

                @pl.when(n == when)
                def _():
                    for k in WAVES[wave]:
                        row_copy(k, part, PATH[k][0]).wait_recv()
                        pass_on(k, part)

        @pl.when(n > 5)
        def _():
            send_lags(n - 4, False)

        @pl.when((n == 4) | (n == 5))
        def _():
            send_lags(n - 4, True)

        v, u, first = half_row(n)

        @pl.loop(0, 2)
        def _(j):
            spectra(n, v, u, first + j, j)

        @pl.when(n % 4 == 3)
        def _():
            total = jnp.zeros((GROUP * 2 * Q, OUT), jnp.float32)
            for k in range(PERIOD // LANES):
                pick = pl.ds(k, GROUP * 2 * Q, stride=8)
                left = jnp.concatenate([ca[pick, :], cb[pick, :]], axis=1).astype(jnp.bfloat16)
                total += jnp.dot(left, table[k], preferred_element_type=jnp.float32)
            at = (n // 4) * GROUP
            stage[pl.ds(at, GROUP)] = total.astype(jnp.bfloat16).reshape(GROUP, 2 * Q, OUT)

    for n in range(steps - 4, steps):
        send_lags(n, False)

    @pl.when(side == band)
    def _():
        pltpu.make_async_copy(stage.at[pr], recv.at[row, band], out_recv).start()

    @pl.when(side != band)
    def _():
        copy = remote(stage.at[pr], recv.at[row, band], twin_send, out_recv, twin)
        copy.start()
        copy.wait_send()

    for copy in pending:
        copy.wait_send()
    for n in range(1, 16):
        for part in (0, 1):
            row_copy(n, part, PATH[n][0]).wait_send()
    pltpu.make_async_copy(
        stage.at[pl.ds(1, blocks - 1)], stage.at[pl.ds(1, blocks - 1)], out_send
    ).wait()
    pltpu.make_async_copy(recv, recv, out_recv).wait()


def unscramble(recv, out, near, wide, in_sem, out_sem):
    to = lax.broadcasted_iota(jnp.int32, (256, 256), 0)
    at = lax.broadcasted_iota(jnp.int32, (256, 256), 1)
    steps = [(s, g) for s in range(2) for g in range(4)]
    takes = []
    for n, (s, g) in enumerate(steps):
        block = pl.ds(8 * g, 8)
        take = pltpu.make_async_copy(recv.at[block, s], near.at[s, block], in_sem.at[n])
        take.start()
        takes.append(take)
    move = ((to % 16) * 16 + to // 16 == at).astype(jnp.bfloat16)
    gives = []
    for n, (s, g) in enumerate(steps):
        takes[n].wait()
        value = near[s, 8 * g : 8 * g + 8].reshape(256, OUT)
        value = jnp.dot(move, value, preferred_element_type=jnp.float32)
        wide[s, :, 16 * g : 16 * g + 16, :] = value.reshape(Q, 16, OUT)
        row = pl.ds(16 * g, 16)
        give = pltpu.make_async_copy(wide.at[s, :, row, :], out.at[s, :, row, :], out_sem.at[n])
        give.start()
        gives.append(give)
    for give in gives:
        give.wait()


def per_device(traces, sources, owner):
    stations = traces.shape[0]
    blocks = lax.axis_size("blk")
    tiles = traces.shape[2] // LANES
    x_in = traces.reshape(stations, 2, tiles, LANES).transpose(0, 2, 1, 3)
    x_in = x_in.reshape(stations, 2 * tiles, LANES)
    s_in = sources.reshape(2, 2, tiles, LANES).transpose(0, 2, 1, 3).reshape(2, 2 * tiles, LANES)
    table = jnp.asarray(lag_table())
    vmem = pl.BlockSpec(memory_space=pltpu.VMEM)
    recv = pl.pallas_call(
        correlate,
        out_shape=jax.ShapeDtypeStruct((blocks // 2, 2, 2 * Q, OUT), jnp.bfloat16),
        in_specs=[
            vmem,
            pl.BlockSpec(memory_space=pl.ANY),
            pl.BlockSpec(memory_space=pl.ANY),
            pl.BlockSpec(memory_space=pl.ANY),
        ],
        out_specs=pl.BlockSpec(memory_space=pl.ANY),
        scratch_shapes=[
            pltpu.VMEM((PERIOD // LANES, 2 * LANES, OUT), jnp.bfloat16),
            pltpu.VMEM((2, LANES), jnp.int32),
            pltpu.SMEM((2, LANES), jnp.int32),
            pltpu.VMEM((8, 2 * ROWS, LANES), jnp.float32),
            pltpu.VMEM((stations, 2 * ROWS, LANES), jnp.bfloat16),
            pltpu.VMEM((stations + 1, 3, ROWS, LANES), jnp.bfloat16),
            pltpu.VMEM((2 * ROWS, LANES), jnp.bfloat16),
            pltpu.VMEM((SIDE, SIDE, SIDE, 2 * ROWS, LANES), jnp.bfloat16),
            pltpu.VMEM((GROUP * 2 * Q * 8, LANES), jnp.float32),
            pltpu.VMEM((GROUP * 2 * Q * 8, LANES), jnp.float32),
            pltpu.VMEM((blocks, 2 * Q, OUT), jnp.bfloat16),
            pltpu.SemaphoreType.DMA((2,)),
            pltpu.SemaphoreType.DMA((2,)),
            pltpu.SemaphoreType.DMA((4,)),
            pltpu.SemaphoreType.DMA((33,)),
            pltpu.SemaphoreType.DMA((33,)),
            pltpu.SemaphoreType.DMA,
            pltpu.SemaphoreType.DMA,
            pltpu.SemaphoreType.DMA,
        ],
        compiler_params=pltpu.CompilerParams(
            has_side_effects=True, collective_id=0, vmem_limit_bytes=52 * 1024 * 1024
        ),
        name="correlate",
    )(owner.reshape(1, stations), x_in, s_in, table)
    return pl.pallas_call(
        unscramble,
        out_shape=jax.ShapeDtypeStruct((2, Q, 64, OUT), jnp.float32),
        in_specs=[pl.BlockSpec(memory_space=pl.ANY)],
        out_specs=pl.BlockSpec(memory_space=pl.ANY),
        scratch_shapes=[
            pltpu.VMEM((2, blocks // 2, 2 * Q, OUT), jnp.bfloat16),
            pltpu.VMEM((2, Q, 64, OUT), jnp.float32),
            pltpu.SemaphoreType.DMA((8,)),
            pltpu.SemaphoreType.DMA((8,)),
        ],
        compiler_params=pltpu.CompilerParams(vmem_limit_bytes=16 * 1024 * 1024),
        name="unscramble",
    )(recv)


def solution(mesh):
    placed = (P("blk", None, "band"), P("blk", None, "band"), P("blk", None))
    return jax.shard_map(
        per_device,
        mesh=mesh,
        in_specs=placed,
        out_specs=P("blk", None, "band", None),
        check_vma=False,
    )
```
